128 devices in a mesh: chan: 8 (over x, core), bl: 16 (over y, z).
Axes of the slice: x: 4, y: 4, z: 4, core: 2. Of those that a mesh axis runs over, the one named last changes fastest.
Arguments:
- visibilities: float32 [2, 128, 32768], P(None, 'chan', 'bl'), may hold values from -6 to 6
- coherencies: float32 [2, 8, 128, 32768], P(None, None, 'chan', 'bl'), may hold values from -0.5 to 0.5
- station_pairs: int32 [2, 32768], P(None, 'bl'), may hold values from 0 to 511, as said below
- gains_start: float32 [512, 2, 8, 128], P('bl', None, None, 'chan'), may hold values from -4 to 4
- consensus_prev: float32 [512, 2, 8, 128], P('bl', None, None, 'chan'), may hold values from -4 to 4
- dual_prev: float32 [512, 2, 8, 128], P('bl', None, None, 'chan'), may hold values from -4 to 4
- penalty: float32 [8], replicated, may hold values from 0.5 to 4
Outputs:
- gains: float32 [512, 2, 8, 128], P('bl', None, None, 'chan')
- consensus: float32 [512, 2, 8, 128], P('bl', None, None, 'chan')
- dual: float32 [512, 2, 8, 128], P('bl', None, None, 'chan')
The draws below stay inside these ranges and needn't reach their ends.
Inputs may be any that keep to these rules, and one draw needn't show every extreme that they name: `station_pairs`: column b names the two stations of baseline b, the first below the second; no pair appears twice.
All inputs are finite; a program needn't handle non-finite values.
Results may differ from the reference program's by a relative error of at most 0.0003.
Values sent between devices are 32-bit elements; how exact they have to be, the bound alone decides.
No kernel may reach another device: no remote copies, remote signals or barrier semaphores. Data moves between devices by JAX's collectives and lax.ppermute only.
A program may use at most 64 MiB of HBM per device.

```python
import math
import jax
import jax.numpy as jnp
from jax import lax

NS = 512
K = 8
PASSES = 2
POLY = 4
NCH = 128
BL_TOTAL = 32768


def draw_station_pairs(key, part):
    total = NS * (NS - 1) // 2
    order = jax.random.permutation(key, total)[:BL_TOTAL]
    upper, lower = jnp.triu_indices(NS, 1)
    return jnp.stack([upper[order], lower[order]]).astype(jnp.int32)


def block_levels(own_key, dims, shards, smallest, high):
    def one(dim, blocks):
        steps = jax.random.uniform(jax.random.fold_in(jax.random.fold_in(own_key, 6), dim), (blocks,), jnp.float32, smallest / len(shards), high / len(shards))
        return jnp.repeat(jnp.exp(steps), dims[dim] // blocks).reshape((-1,) + (1,) * (len(dims) - dim - 1))

    gain = one(*shards[0])
    for cut in shards[1:]:
        gain = gain * one(*cut)
    return gain


def bell_draw(stream_key, dims, deviation, limit, cuts=(), dtype=jnp.bfloat16):
    values = deviation * jax.random.normal(stream_key, dims, jnp.float32)
    if cuts:
        values = values * block_levels(stream_key, dims, cuts, -0.22, 0.18)
    return jnp.clip(values, -limit, limit).astype(dtype)


def setup_inputs(seed: int = 0) -> dict:
    key_list = jax.random.split(jax.random.key(seed), 8)
    return {
        "visibilities": bell_draw(key_list[0], (2, NCH, BL_TOTAL), 0.4, 6.0, ((1, 8), (2, 16)), jnp.float32),
        "coherencies": bell_draw(key_list[1], (2, K, NCH, BL_TOTAL), (2 * BL_TOTAL // NS) ** -0.5, 0.5, ((2, 8), (3, 16)), jnp.float32),
        "station_pairs": draw_station_pairs(jax.random.fold_in(key_list[7], 71), 0),
        "gains_start": bell_draw(key_list[3], (NS, 2, K, NCH), 0.7, 4.0, ((0, 16), (3, 8)), jnp.float32),
        "consensus_prev": bell_draw(key_list[4], (NS, 2, K, NCH), 0.7, 4.0, ((0, 16), (3, 8)), jnp.float32),
        "dual_prev": bell_draw(key_list[5], (NS, 2, K, NCH), 0.3, 4.0, ((0, 16), (3, 8)), jnp.float32),
        "penalty": jnp.clip(jnp.exp(jax.random.uniform(key_list[6], (K,), jnp.float32, math.log(0.5), math.log(4.0))), 0.5, 4.0),
    }


def poly_basis(count, order):
    freq = 2.0 * (jnp.arange(count).astype(jnp.float32) + 0.5) / count - 1.0
    columns = []
    for power in range(order):
        vector = freq ** power
        for before in columns:
            vector = vector - jnp.sum(before * vector) * before
        vector = vector / jnp.sqrt(jnp.sum(vector * vector))
        columns.append(vector)
    return jnp.stack(columns, axis=1)

def reference(visibilities, coherencies, station_pairs, gains_start, consensus_prev, dual_prev, penalty):
    first = station_pairs[0]
    second = station_pairs[1]
    mu_dir = 0.5 * penalty
    vis_chan = jnp.moveaxis(visibilities, 1, 0)
    coh_chan = jnp.moveaxis(coherencies, 2, 0)
    cons_chan = jnp.moveaxis(consensus_prev, 3, 0)
    dual_chan = jnp.moveaxis(dual_prev, 3, 0)

    def one_channel(items):
        vis_one, coh_one, gain_one, cons_one, dual_one = items
        table = jnp.transpose(gain_one, (1, 2, 0))
        gain_p = jnp.take(table, first, axis=2)
        gain_q = jnp.take(table, second, axis=2)
        coh_re, coh_im = (coh_one[0], coh_one[1])
        far_re = coh_re * gain_q[0] + coh_im * gain_q[1]
        far_im = coh_im * gain_q[0] - coh_re * gain_q[1]
        model_re = gain_p[0] * far_re - gain_p[1] * far_im
        model_im = gain_p[0] * far_im + gain_p[1] * far_re
        resid_re = vis_one[0] - lax.optimization_barrier(jnp.sum(model_re, axis=0))
        resid_im = vis_one[1] - lax.optimization_barrier(jnp.sum(model_im, axis=0))
        rest_re = resid_re[None] + model_re
        rest_im = resid_im[None] + model_im
        near_re = coh_re * gain_p[0] - coh_im * gain_p[1]
        near_im = coh_re * gain_p[1] + coh_im * gain_p[0]
        side_p = jnp.stack([far_re * rest_re + far_im * rest_im, far_re * rest_im - far_im * rest_re, far_re * far_re + far_im * far_im])
        side_q = jnp.stack([near_re * rest_re + near_im * rest_im, near_im * rest_re - near_re * rest_im, near_re * near_re + near_im * near_im])
        totals = jax.ops.segment_sum(jnp.moveaxis(side_p, 2, 0), first, num_segments=NS)
        totals = totals + jax.ops.segment_sum(jnp.moveaxis(side_q, 2, 0), second, num_segments=NS)
        denom = totals[:, 2] + mu_dir[None, :]
        new_re = (totals[:, 0] + mu_dir[None, :] * cons_one[:, 0] - 0.5 * dual_one[:, 0]) / denom
        new_im = (totals[:, 1] + mu_dir[None, :] * cons_one[:, 1] - 0.5 * dual_one[:, 1]) / denom
        return jnp.stack([new_re, new_im], axis=1)
    gain_chan = jnp.moveaxis(gains_start, 3, 0)
    for gain_pass in range(PASSES):
        gain_chan = lax.map(one_channel, (vis_chan, coh_chan, gain_chan, cons_chan, dual_chan))
    gains = jnp.moveaxis(gain_chan, 0, 3)
    basis = poly_basis(NCH, POLY)
    rho_b = penalty[None, None, :, None]
    target = gains + dual_prev / rho_b
    coef = jnp.einsum('sjkc,cm->sjkm', target, basis, precision=lax.Precision.HIGHEST)
    consensus = jnp.einsum('sjkm,cm->sjkc', coef, basis, precision=lax.Precision.HIGHEST)
    dual = dual_prev + rho_b * (gains - consensus)
    return (gains, consensus, dual)
```

```python
import functools

import jax
import jax.numpy as jnp
import numpy as np
from jax import lax
from jax.experimental import pallas as pl
from jax.experimental.pallas import tpu as pltpu
from jax.sharding import PartitionSpec as P

PASSES = 2
POLY = 4
CHUNK = 256
VMEM = pl.BlockSpec(memory_space=pltpu.VMEM)
SMEM = pl.BlockSpec(memory_space=pltpu.SMEM)
LIMIT = pltpu.CompilerParams(vmem_limit_bytes=48 * 1024 * 1024)


def poly_basis(count, order):
    freq = 2.0 * (np.arange(count).astype(np.float64) + 0.5) / count - 1.0
    columns = []
    for power in range(order):
        vector = freq**power
        for before in columns:
            vector = vector - np.sum(before * vector) * before
        columns.append(vector / np.sqrt(np.sum(vector * vector)))
    return np.stack(columns, axis=1).astype(np.float32)


def spread(block, out_ref):
    for part in range(out_ref.shape[0]):
        out_ref[part] = block


def prep_kernel(gain_ref, out_ref):
    spread(gain_ref[...].T, out_ref)


def pass_kernel(dims, pairs_ref, table_ref, vis_ref, coh_ref, out_ref, table_scr, sums_scr):
    stations, directions, chans, lanes = dims
    rows = directions * chans
    width = 2 * rows
    flat = table_ref[...].reshape(stations, width).T
    upper = flat.astype(jnp.bfloat16)
    table_scr[0:width] = upper
    table_scr[width : 2 * width] = (flat - upper.astype(jnp.float32)).astype(jnp.bfloat16)
    labels = lax.broadcasted_iota(jnp.int32, (stations, CHUNK), 0)
    for chunk in range(lanes // CHUNK):
        cut = pl.ds(chunk * CHUNK, CHUNK)
        onehots = []
        gains = []
        for side in range(2):
            onehot = jnp.where(labels == pairs_ref[side : side + 1, cut], 1.0, 0.0)
            onehot = onehot.astype(jnp.bfloat16)
            both = jnp.dot(table_scr[...], onehot, preferred_element_type=jnp.float32)
            picked = both[0:width] + both[width : 2 * width]
            gains.append(picked.reshape(2, directions, chans, CHUNK))
            onehots.append(onehot)
        (gp_re, gp_im), (gq_re, gq_im) = gains
        coh_re = coh_ref[0, :, :, cut]
        coh_im = coh_ref[1, :, :, cut]
        cross_re = gp_re * gq_re + gp_im * gq_im
        cross_im = gp_im * gq_re - gp_re * gq_im
        model_re = coh_re * cross_re - coh_im * cross_im
        model_im = coh_re * cross_im + coh_im * cross_re
        res_re = (vis_ref[0, :, cut] - jnp.sum(model_re, axis=0))[None]
        res_im = (vis_ref[1, :, cut] - jnp.sum(model_im, axis=0))[None]
        turn_re = coh_re * res_re + coh_im * res_im
        turn_im = coh_re * res_im - coh_im * res_re
        power = coh_re * coh_re + coh_im * coh_im
        side_p = [
            turn_re * gq_re - turn_im * gq_im,
            turn_re * gq_im + turn_im * gq_re,
            power * (gq_re * gq_re + gq_im * gq_im),
        ]
        side_q = [
            turn_re * gp_re + turn_im * gp_im,
            turn_re * gp_im - turn_im * gp_re,
            power * (gp_re * gp_re + gp_im * gp_im),
        ]
        uppers = []
        lowers = []
        for terms in (side_p, side_q):
            whole = jnp.concatenate([t.reshape(rows, CHUNK) for t in terms], axis=0)
            upper = whole.astype(jnp.bfloat16)
            uppers.append(upper)
            lowers.append((whole - upper.astype(jnp.float32)).astype(jnp.bfloat16))
        terms = jnp.concatenate(
            [jnp.concatenate(uppers, axis=1), jnp.concatenate(lowers, axis=1)], axis=0
        )
        part = lax.dot_general(
            jnp.concatenate(onehots, axis=1),
            terms,
            (((1,), (1,)), ((), ())),
            preferred_element_type=jnp.float32,
        )
        if chunk == 0:
            sums_scr[...] = part
        else:
            sums_scr[...] += part
    out_ref[...] = (sums_scr[:, 0 : 3 * rows] + sums_scr[:, 3 * rows :]).reshape(out_ref.shape)


def per_lane(penalty_ref, directions, chans):
    lane = lax.broadcasted_iota(jnp.int32, (1, directions * chans), 1) // chans
    row = jnp.zeros((1, directions * chans), jnp.float32)
    for k in range(directions):
        row = jnp.where(lane == k, penalty_ref[k], row)
    return row


def solve(penalty_ref, sums_ref, gain_ref, cons_ref, dual_ref, directions, chans):
    rows = directions * chans
    mu = 0.5 * per_lane(penalty_ref, directions, chans)
    sums = jnp.sum(sums_ref[...], axis=0)
    cons = cons_ref[...].T
    dual = dual_ref[...].T
    power = sums[:, 2 * rows :]
    fresh = []
    for part in range(2):
        cut = slice(part * rows, (part + 1) * rows)
        top = sums[:, cut] + gain_ref[:, cut] * power + mu * cons[:, cut] - 0.5 * dual[:, cut]
        fresh.append(top / (power + mu))
    return jnp.concatenate(fresh, axis=1)


def update_kernel(dims, penalty_ref, sums_ref, gain_ref, cons_ref, dual_ref, out_ref):
    spread(solve(penalty_ref, sums_ref, gain_ref, cons_ref, dual_ref, *dims), out_ref)


def pack(block):
    depth = block.shape[0] * block.shape[1] // 128
    return jnp.concatenate(
        [block[first : first + depth] for first in range(0, block.shape[0], depth)], axis=1
    )


def unpack(block, lanes):
    return jnp.concatenate(
        [block[:, first : first + lanes] for first in range(0, 128, lanes)], axis=0
    )


def fit_kernel(
    dims, penalty_ref, basis_ref, sums_ref, gain_ref, cons_ref, dual_ref, gain_out, coef_ref
):
    directions, chans = dims
    gain = solve(penalty_ref, sums_ref, gain_ref, cons_ref, dual_ref, directions, chans).T
    gain_out[...] = gain
    coefs = []
    for part in range(2 * directions):
        cut = slice(part * chans, (part + 1) * chans)
        target = gain[cut] + dual_ref[cut] / penalty_ref[part % directions]
        for m in range(POLY):
            coefs.append(jnp.sum(target * basis_ref[:, m : m + 1], axis=0, keepdims=True))
    spread(pack(jnp.concatenate(coefs, axis=0)), coef_ref)


def finish_kernel(
    dims, penalty_ref, basis_ref, coef_ref, gain_ref, dual_ref, cons_out, dual_out
):
    directions, chans = dims
    coef = unpack(jnp.sum(coef_ref[...], axis=0), gain_ref.shape[1])
    for part in range(2 * directions):
        cut = slice(part * chans, (part + 1) * chans)
        cons = coef[part * POLY : part * POLY + 1] * basis_ref[:, 0:1]
        for m in range(1, POLY):
            cons += coef[part * POLY + m : part * POLY + m + 1] * basis_ref[:, m : m + 1]
        cons_out[cut] = cons
        dual_out[cut] = dual_ref[cut] + penalty_ref[part % directions] * (gain_ref[cut] - cons)


def local(
    visibilities, coherencies, station_pairs, gains_start, consensus_prev, dual_prev, penalty
):
    owned, _, directions, chans = gains_start.shape
    lanes = visibilities.shape[2]
    parts = lax.axis_size("bl")
    groups = lax.axis_size("chan")
    stations = owned * parts
    rows = directions * chans
    width = 2 * rows
    dims = (directions, chans)

    def flat(array):
        return jnp.transpose(array, (1, 2, 3, 0)).reshape(width, owned)

    def call(kernel, shapes, specs, **extra):
        return pl.pallas_call(
            kernel,
            out_shape=[jax.ShapeDtypeStruct(s, jnp.float32) for s in shapes],
            in_specs=specs,
            out_specs=[VMEM] * len(shapes),
            compiler_params=LIMIT,
            **extra,
        )

    gain_rows, cons_rows, dual_rows = flat(gains_start), flat(consensus_prev), flat(dual_prev)
    basis = jnp.asarray(poly_basis(chans * groups, POLY))
    mine = lax.dynamic_slice_in_dim(basis, lax.axis_index("chan") * chans, chans, 0)
    (copies,) = call(prep_kernel, [(parts, owned, width)], [VMEM])(gain_rows)
    for gain_pass in range(PASSES):
        table = lax.all_to_all(copies, "bl", 0, 0, tiled=True)
        (sums,) = call(
            functools.partial(pass_kernel, (stations, directions, chans, lanes)),
            [(parts, owned, 3 * rows)],
            [VMEM] * 4,
            scratch_shapes=[
                pltpu.VMEM((2 * width, stations), jnp.bfloat16),
                pltpu.VMEM((stations, 6 * rows), jnp.float32),
            ],
        )(station_pairs, table, visibilities, coherencies)
        sums = lax.all_to_all(sums, "bl", 0, 0, tiled=True)
        own = copies[0]
        if gain_pass < PASSES - 1:
            (copies,) = call(
                functools.partial(update_kernel, dims),
                [(parts, owned, width)],
                [SMEM] + [VMEM] * 4,
            )(penalty, sums, own, cons_rows, dual_rows)
    gain, coef = call(
        functools.partial(fit_kernel, dims),
        [(width, owned), (groups, 2 * directions * POLY * owned // 128, 128)],
        [SMEM] + [VMEM] * 5,
    )(penalty, mine, sums, own, cons_rows, dual_rows)
    coef = lax.all_to_all(coef, "chan", 0, 0, tiled=True)
    cons, dual = call(
        functools.partial(finish_kernel, dims),
        [(width, owned), (width, owned)],
        [SMEM] + [VMEM] * 4,
    )(penalty, mine, coef, gain, dual_rows)

    def back(array):
        return jnp.transpose(array.reshape(2, directions, chans, owned), (3, 0, 1, 2))

    return (back(gain), back(cons), back(dual))


def solution(mesh):
    placed = (
        P(None, "chan", "bl"),
        P(None, None, "chan", "bl"),
        P(None, "bl"),
        P("bl", None, None, "chan"),
        P("bl", None, None, "chan"),
        P("bl", None, None, "chan"),
        P(),
    )
    return jax.shard_map(
        local,
        mesh=mesh,
        in_specs=placed,
        out_specs=(
            P("bl", None, None, "chan"),
            P("bl", None, None, "chan"),
            P("bl", None, None, "chan"),
        ),
        check_vma=False,
    )
```

```python
import functools

import jax
import jax.numpy as jnp
import numpy as np
from jax import lax
from jax.experimental import pallas as pl
from jax.experimental.pallas import tpu as pltpu
from jax.sharding import PartitionSpec as P

PASSES = 2
POLY = 4
LANE = 128
GROUP = 1
UNROLL = 4
VMEM = pl.BlockSpec(memory_space=pltpu.VMEM)
SMEM = pl.BlockSpec(memory_space=pltpu.SMEM)
HBM = pl.BlockSpec(memory_space=pltpu.HBM)
LIMIT = pltpu.CompilerParams(vmem_limit_bytes=40 * 1024 * 1024)


def poly_basis(count, order):
    freq = 2.0 * (np.arange(count).astype(np.float64) + 0.5) / count - 1.0
    columns = []
    for power in range(order):
        vector = freq**power
        for before in columns:
            vector = vector - np.sum(before * vector) * before
        columns.append(vector / np.sqrt(np.sum(vector * vector)))
    return np.stack(columns, axis=1).astype(np.float32)


def prep_kernel(dims, vis_hbm, coh_hbm, pairs_hbm, *rest):
    directions, chans, start, tiles, owned, with_own = dims
    if with_own:
        gain_hbm, cons_hbm, dual_hbm, out_ref, coh_scr, vis_scr, pairs_scr, sems, own_scr, all_scr = rest
    else:
        out_ref, coh_scr, vis_scr, pairs_scr, sems = rest
    base = tiles * 2 * directions
    copies = [pltpu.make_async_copy(pairs_hbm, pairs_scr, sems.at[2 * tiles])]
    if with_own:
        for i, ref in enumerate((gain_hbm, cons_hbm, dual_hbm)):
            copies.append(pltpu.make_async_copy(ref, own_scr.at[i], sems.at[2 * tiles + 1 + i]))
    vis_copies = []
    coh_copies = []
    for tile in range(tiles):
        cut = pl.ds((start + tile) * LANE, LANE)
        coh_copies.append(
            pltpu.make_async_copy(coh_hbm.at[:, cut], coh_scr.at[tile], sems.at[tile])
        )
        vis_copies.append(
            pltpu.make_async_copy(
                vis_hbm.at[:, :, cut],
                vis_scr.at[:, pl.ds(tile * chans, chans)],
                sems.at[tiles + tile],
            )
        )
    for copy in copies + coh_copies + vis_copies:
        copy.start()
    for copy in copies:
        copy.wait()
    if with_own:
        own = [own_scr[i] for i in range(3)]
        all_scr[...] = jnp.concatenate(own + [jnp.zeros_like(own[0])], axis=1)
        for chan in range(chans):
            rows = pl.ds(chan, 2 * directions, stride=chans)
            out_ref[chan, pl.ds(base + 4 * tiles, 2 * directions)] = all_scr[rows, :]
    for tile in range(tiles):
        for side in range(2):
            row = pairs_scr[side : side + 1, pl.ds((start + tile) * LANE, LANE)]
            row = row.astype(jnp.float32)
            for chan in range(chans):
                out_ref[chan, pl.ds(base + (2 + side) * tiles + tile, 1)] = row
    for tile in range(tiles):
        coh_copies[tile].wait()
        for chan in range(chans):
            for part in range(2):
                out_ref[chan, pl.ds((2 * tile + part) * directions, directions)] = coh_scr[
                    tile, pl.ds(part * directions * chans + chan, directions, stride=chans)
                ]
    for copy in vis_copies:
        copy.wait()
    for chan in range(chans):
        for part in range(2):
            out_ref[chan, pl.ds(base + part * tiles, tiles)] = vis_scr[
                part, pl.ds(chan, tiles, stride=chans)
            ]


def pick(tables, low, highs):
    out = None
    for index, table in enumerate(tables):
        found = jnp.take_along_axis(table, low, axis=1)
        out = found if index == 0 else jnp.where(highs[index], found, out)
    return out


def split_pack(re, im, power):
    pair = jnp.concatenate([re, im], axis=0)
    upper = pair.astype(jnp.bfloat16)
    lower = (pair - upper.astype(jnp.float32)).astype(jnp.bfloat16)
    rest = power - power.astype(jnp.bfloat16).astype(jnp.float32)
    last = jnp.concatenate([power, rest], axis=0).astype(jnp.bfloat16)
    return upper, lower, last


def per_direction(penalty_ref, shape, period):
    row = (lax.broadcasted_iota(jnp.int32, shape, 0) // period) % penalty_ref.shape[0]
    rho = jnp.zeros(shape, jnp.float32)
    for k in range(penalty_ref.shape[0]):
        rho = jnp.where(row == k, penalty_ref[k], rho)
    return rho


class Sweep:
    def __init__(self, dims, x_ref, pair_scr, sums_scr):
        self.directions, self.tiles, self.stations, self.parts = dims
        self.x_ref, self.pair_scr, self.sums_scr = x_ref, pair_scr, sums_scr
        self.first = self.tiles * 2 * self.directions

    def index(self):
        tiles = self.tiles
        for part in range(self.parts):
            whole = self.x_ref[part, pl.ds(self.first + 2 * tiles, 2 * tiles)].astype(jnp.int32)
            self.pair_scr[part, pl.ds(0, 2 * tiles)] = jnp.bitwise_and(whole, LANE - 1)
            self.pair_scr[part, pl.ds(2 * tiles, 2 * tiles)] = jnp.right_shift(whole, 7)

    def fill(self, part, tables):
        directions, tiles, first = self.directions, self.tiles, self.first
        x_ref, pair_scr = self.x_ref, self.pair_scr
        stripes = self.stations // LANE
        depth = 6 * directions
        wide = (LANE // 16, 16, LANE)
        labels = lax.broadcasted_iota(jnp.int32, (LANE, LANE), 0).astype(jnp.float32)
        labels = labels.astype(jnp.bfloat16).reshape(wide)
        one, zero = jnp.ones(wide, jnp.bfloat16), jnp.zeros(wide, jnp.bfloat16)

        def twice(rows):
            return jnp.concatenate([rows, rows], axis=0).astype(jnp.bfloat16)

        def rows16(row):
            return jnp.broadcast_to(row.astype(jnp.float32), (16, LANE)).astype(jnp.bfloat16)

        lefts, rights = [], []
        for tile in range(tiles):
            gains = []
            masks = []
            for side in range(2):
                low = pair_scr[part, pl.ds(side * tiles + tile, 1)]
                high = pair_scr[part, pl.ds((2 + side) * tiles + tile, 1)]
                low8 = jnp.broadcast_to(low, (directions, LANE))
                high8 = jnp.broadcast_to(high, (directions, LANE))
                highs = [high8 == s for s in range(stripes)]
                gains.append([pick(tables[j], low8, highs) for j in range(2)])
                masks.append([twice(jnp.where(h, 1.0, 0.0)) for h in highs])
                hot = jnp.where(labels == rows16(low)[None], one, zero)
                rights.append(hot.reshape(LANE, LANE))
            (gp_re, gp_im), (gq_re, gq_im) = gains
            coh_re, coh_im = [
                x_ref[part, pl.ds((2 * tile + j) * directions, directions)] for j in range(2)
            ]
            cross_re = gp_re * gq_re + gp_im * gq_im
            cross_im = gp_im * gq_re - gp_re * gq_im
            model_re = coh_re * cross_re - coh_im * cross_im
            model_im = coh_re * cross_im + coh_im * cross_re
            res_re = x_ref[part, pl.ds(first + tile, 1)] - jnp.sum(model_re, axis=0, keepdims=True)
            res_im = x_ref[part, pl.ds(first + tiles + tile, 1)] - jnp.sum(
                model_im, axis=0, keepdims=True
            )
            turn_re = coh_re * res_re + coh_im * res_im
            turn_im = coh_re * res_im - coh_im * res_re
            power = coh_re * coh_re + coh_im * coh_im
            terms_p = split_pack(
                turn_re * gq_re - turn_im * gq_im,
                turn_re * gq_im + turn_im * gq_re,
                power * (gq_re * gq_re + gq_im * gq_im),
            )
            terms_q = split_pack(
                turn_re * gp_re + turn_im * gp_im,
                turn_re * gp_im - turn_im * gp_re,
                power * (gp_re * gp_re + gp_im * gp_im),
            )
            for side, terms in enumerate((terms_p, terms_q)):
                both = jnp.stack(terms)
                lefts.append(
                    jnp.concatenate(
                        [
                            (both * masks[side][s][None]).reshape(depth, LANE)
                            for s in range(stripes)
                        ],
                        axis=0,
                    )
                )
            if (tile + 1) % GROUP == 0:
                self.sums_scr[...] += lax.dot_general(
                    jnp.concatenate(lefts, axis=1),
                    jnp.concatenate(rights, axis=1),
                    (((1,), (1,)), ((), ())),
                    preferred_element_type=jnp.float32,
                )
                lefts, rights = [], []

    def run(self, tables):
        @pl.loop(0, self.parts // UNROLL)
        def _(step):
            for i in range(UNROLL):
                self.fill(UNROLL * step + i, tables)


def read_tables(table_scr, stations):
    return [
        [table_scr[j, :, pl.ds(s * LANE, LANE)] for s in range(stations // LANE)]
        for j in range(2)
    ]


def own_rows(x_ref, at, owned, parts, directions):
    own = [x_ref[part, pl.ds(at, 2 * directions)] for part in range(parts)]
    return [
        jnp.concatenate([block[:, i * owned : (i + 1) * owned] for block in own], axis=1)
        for i in range(3)
    ]


def main_kernel(
    dims, owned, groups, penalty_ref, x_ref, out_ref, table_scr, base_scr, pair_scr, sums_scr
):
    directions, tiles, stations, parts = dims
    stripes = stations // LANE
    depth = 6 * directions
    rho = per_direction(penalty_ref, (directions, 1), 1)
    mu = 0.5 * rho

    gain, cons, dual = own_rows(x_ref, tiles * (2 * directions + 4), owned, parts, directions)
    for j in range(2):
        cut = slice(j * directions, (j + 1) * directions)
        table_scr[j] = gain[cut]
        base_scr[j] = mu * cons[cut] - 0.5 * dual[cut]
        base_scr[2 + j] = dual[cut] / rho
    sweep = Sweep(dims, x_ref, pair_scr, sums_scr)
    sweep.index()

    for gain_pass in range(PASSES):
        tables = read_tables(table_scr, stations)
        sums_scr[...] = jnp.zeros_like(sums_scr)
        sweep.run(tables)
        for s in range(stripes):
            cut = pl.ds(s * LANE, LANE)
            block = sums_scr[pl.ds(s * depth, depth)]
            total = block[0 : 2 * directions] + block[2 * directions : 4 * directions]
            power = block[4 * directions : 5 * directions] + block[5 * directions :]
            for j in range(2):
                top = total[j * directions : (j + 1) * directions]
                top = top + table_scr[j, :, cut] * power + base_scr[j, :, cut]
                table_scr[j, :, cut] = top / (power + mu)

    half = directions // 2
    for part in range(parts):
        cut = pl.ds(part * owned, owned)
        pieces = []
        for j in range(2):
            target = table_scr[j, :, cut] + base_scr[2 + j, :, cut]
            pieces += [target[0:half], target[half:]]
        block = jnp.concatenate(pieces, axis=1)
        for group in range(groups):
            out_ref[group * parts + part] = block


def finish_kernel(
    dims, penalty_ref, basis_ref, x_ref, dual_ref, gain_out, cons_out, dual_out, out_scr
):
    directions, chans, owned, count = dims
    half = directions // 2
    start = lax.axis_index("chan") * chans
    coefs = [jnp.zeros((half, LANE), jnp.float32) for _ in range(POLY)]
    for channel in range(count):
        block = x_ref[channel]
        for m in range(POLY):
            coefs[m] = coefs[m] + block * basis_ref[channel * POLY + m]
    for chan in range(chans):
        block = x_ref[start + chan]
        cons = coefs[0] * basis_ref[(start + chan) * POLY]
        for m in range(1, POLY):
            cons = cons + coefs[m] * basis_ref[(start + chan) * POLY + m]
        for j in range(2):
            rows = pl.ds(j * directions * chans + chan, directions, stride=chans)
            pieces = []
            for source in (block, cons):
                cuts = [source[:, (2 * j + h) * owned : (2 * j + h + 1) * owned] for h in range(2)]
                pieces.append(jnp.concatenate(cuts, axis=0))
            out_scr[rows, :] = jnp.concatenate(pieces + pieces, axis=1)
    whole = out_scr[...]
    rho = per_direction(penalty_ref, (2 * directions * chans, 1), chans)
    dual = dual_ref[...]
    gain = whole[:, 0:owned] - dual / rho
    cons = whole[:, owned : 2 * owned]
    gain_out[...] = gain
    cons_out[...] = cons
    dual_out[...] = dual + rho * (gain - cons)


def local(
    visibilities, coherencies, station_pairs, gains_start, consensus_prev, dual_prev, penalty
):
    owned, _, directions, chans = gains_start.shape
    lanes = visibilities.shape[2]
    parts = lax.axis_size("bl")
    groups = lax.axis_size("chan")
    stations = owned * parts
    tiles = lanes // LANE
    rows = directions * chans
    width = 2 * rows
    depth = 6 * directions * (stations // LANE)

    def flat(array):
        return jnp.transpose(array, (1, 2, 3, 0)).reshape(width, owned)

    def call(kernel, shapes, specs, limit=LIMIT, **extra):
        return pl.pallas_call(
            kernel,
            out_shape=[jax.ShapeDtypeStruct(s, jnp.float32) for s in shapes],
            in_specs=specs,
            out_specs=[VMEM] * len(shapes),
            compiler_params=limit,
            **extra,
        )

    own = (flat(gains_start), flat(consensus_prev), flat(dual_prev))
    basis = jnp.asarray(poly_basis(chans * groups, POLY).reshape(-1))

    def prep(start, span, own):
        count = span * (2 * directions + 4) + (2 * directions if own else 0)
        scratch = [
            pltpu.VMEM((span, width, LANE), jnp.float32),
            pltpu.VMEM((2, span * chans, LANE), jnp.float32),
            pltpu.VMEM(station_pairs.shape, jnp.int32),
            pltpu.SemaphoreType.DMA((2 * span + 4,)),
        ]
        if own:
            scratch.append(pltpu.VMEM((3, width, owned), jnp.float32))
            scratch.append(pltpu.VMEM((width, LANE), jnp.float32))
        dims = (directions, chans, start, span, owned, bool(own))
        return call(
            functools.partial(prep_kernel, dims),
            [(chans, count, LANE)],
            [HBM] * (3 + len(own)),
            limit=pltpu.CompilerParams(),
            scratch_shapes=scratch,
        )(visibilities, coherencies.reshape(width, lanes), station_pairs, *own)[0]

    x = lax.all_to_all(prep(0, tiles, own), "bl", 0, 0, tiled=True)
    dims = (directions, tiles, stations, parts)
    (sent,) = call(
        functools.partial(main_kernel, dims, owned, groups),
        [(groups * parts, directions // 2, LANE)],
        [SMEM, VMEM],
        scratch_shapes=[
            pltpu.VMEM((2, directions, stations), jnp.float32),
            pltpu.VMEM((4, directions, stations), jnp.float32),
            pltpu.VMEM((parts, 4 * tiles, LANE), jnp.int32),
            pltpu.VMEM((depth, LANE), jnp.float32),
        ],
    )(penalty, x)
    held = lax.all_to_all(sent, ("chan", "bl"), 0, 0, tiled=True)
    outs = call(
        functools.partial(finish_kernel, (directions, chans, owned, chans * groups)),
        [(width, owned)] * 3,
        [SMEM, SMEM, VMEM, VMEM],
        scratch_shapes=[pltpu.VMEM((width, LANE), jnp.float32)],
    )(penalty, basis, held, own[2])

    def back(array):
        return jnp.transpose(array.reshape(2, directions, chans, owned), (3, 0, 1, 2))

    return tuple(back(array) for array in outs)


def solution(mesh):
    placed = (
        P(None, "chan", "bl"),
        P(None, None, "chan", "bl"),
        P(None, "bl"),
        P("bl", None, None, "chan"),
        P("bl", None, None, "chan"),
        P("bl", None, None, "chan"),
        P(),
    )
    return jax.shard_map(
        local,
        mesh=mesh,
        in_specs=placed,
        out_specs=(
            P("bl", None, None, "chan"),
            P("bl", None, None, "chan"),
            P("bl", None, None, "chan"),
        ),
        check_vma=False,
    )
```

```python
import functools

import jax
import jax.numpy as jnp
import numpy as np
from jax import lax
from jax.experimental import pallas as pl
from jax.experimental.pallas import tpu as pltpu
from jax.sharding import PartitionSpec as P

PASSES = 2
POLY = 4
LANE = 128
GROUP = 1
UNROLL = 8
VMEM = pl.BlockSpec(memory_space=pltpu.VMEM)
SMEM = pl.BlockSpec(memory_space=pltpu.SMEM)
HBM = pl.BlockSpec(memory_space=pltpu.HBM)
LIMIT = pltpu.CompilerParams(vmem_limit_bytes=40 * 1024 * 1024)


def poly_basis(count, order):
    freq = 2.0 * (np.arange(count).astype(np.float64) + 0.5) / count - 1.0
    columns = []
    for power in range(order):
        vector = freq**power
        for before in columns:
            vector = vector - np.sum(before * vector) * before
        columns.append(vector / np.sqrt(np.sum(vector * vector)))
    return np.stack(columns, axis=1).astype(np.float32)


def prep_kernel(
    dims,
    vis_hbm,
    coh_hbm,
    pairs_hbm,
    gain_hbm,
    cons_hbm,
    dual_hbm,
    out_hbm,
    coh_scr,
    vis_scr,
    pairs_scr,
    own_scr,
    all_scr,
    out_scr,
    sems,
    out_sems,
):
    directions, chans, tiles, owned = dims
    depth = 2 * directions
    base = tiles * depth
    copies = [pltpu.make_async_copy(pairs_hbm, pairs_scr, sems.at[2 * tiles])]
    for i, ref in enumerate((gain_hbm, cons_hbm, dual_hbm)):
        copies.append(pltpu.make_async_copy(ref, own_scr.at[i], sems.at[2 * tiles + 1 + i]))
    vis_copies = []
    coh_copies = []
    for tile in range(tiles):
        cut = pl.ds(tile * LANE, LANE)
        coh_copies.append(
            pltpu.make_async_copy(coh_hbm.at[:, cut], coh_scr.at[tile], sems.at[tile])
        )
        vis_copies.append(
            pltpu.make_async_copy(
                vis_hbm.at[:, :, cut],
                vis_scr.at[:, pl.ds(tile * chans, chans)],
                sems.at[tiles + tile],
            )
        )
    for copy in copies + coh_copies + vis_copies:
        copy.start()
    for copy in copies:
        copy.wait()
    own = [own_scr[i] for i in range(3)]
    all_scr[...] = jnp.concatenate(own + [jnp.zeros_like(own[0])], axis=1)
    for chan in range(chans):
        rows = pl.ds(chan, depth, stride=chans)
        out_scr[chan, pl.ds(base + 4 * tiles, depth)] = all_scr[rows, :]
    for side in range(2):
        for tile in range(tiles):
            row = pairs_scr[side : side + 1, pl.ds(tile * LANE, LANE)].astype(jnp.float32)
            all_scr[pl.ds(side * tiles + tile, 1), :] = row
    pairs = all_scr[pl.ds(0, 2 * tiles)]
    for chan in range(chans):
        out_scr[chan, pl.ds(base + 2 * tiles, 2 * tiles)] = pairs
    out_copies = []

    def send(first, rows):
        cut = pl.ds(first, rows)
        copy = pltpu.make_async_copy(
            out_scr.at[:, cut], out_hbm.at[:, cut], out_sems.at[len(out_copies)]
        )
        copy.start()
        out_copies.append(copy)

    for tile in range(tiles):
        coh_copies[tile].wait()
        for chan in range(chans):
            for part in range(2):
                out_scr[chan, pl.ds((2 * tile + part) * directions, directions)] = coh_scr[
                    tile, pl.ds(part * directions * chans + chan, directions, stride=chans)
                ]
        if tile % 2:
            send((tile - 1) * depth, 2 * depth)
    for copy in vis_copies:
        copy.wait()
    for chan in range(chans):
        for part in range(2):
            out_scr[chan, pl.ds(base + part * tiles, tiles)] = vis_scr[
                part, pl.ds(chan, tiles, stride=chans)
            ]
    send(base, 4 * tiles + depth)
    for copy in out_copies:
        copy.wait()


def pick(tables, low, highs):
    out = None
    for index, table in enumerate(tables):
        found = jnp.take_along_axis(table, low, axis=1)
        out = found if index == 0 else jnp.where(highs[index], found, out)
    return out


def split_pack(re, im, power):
    pair = jnp.concatenate([re, im], axis=0)
    upper = pair.astype(jnp.bfloat16)
    lower = (pair - upper.astype(jnp.float32)).astype(jnp.bfloat16)
    rest = power - power.astype(jnp.bfloat16).astype(jnp.float32)
    last = jnp.concatenate([power, rest], axis=0).astype(jnp.bfloat16)
    return upper, lower, last


def per_direction(penalty_ref, shape, period):
    row = (lax.broadcasted_iota(jnp.int32, shape, 0) // period) % penalty_ref.shape[0]
    rho = jnp.zeros(shape, jnp.float32)
    for k in range(penalty_ref.shape[0]):
        rho = jnp.where(row == k, penalty_ref[k], rho)
    return rho


class Sweep:
    def __init__(self, dims, x_ref, pair_scr, float_scr, sums_scr):
        self.directions, self.tiles, self.stations, self.parts = dims
        self.x_ref, self.sums_scr = x_ref, sums_scr
        self.pair_scr, self.float_scr = pair_scr, float_scr
        self.first = self.tiles * 2 * self.directions

    def index(self):
        tiles = self.tiles
        for part in range(self.parts):
            whole = self.x_ref[part, pl.ds(self.first + 2 * tiles, 2 * tiles)].astype(jnp.int32)
            low, high = jnp.bitwise_and(whole, LANE - 1), jnp.right_shift(whole, 7)
            self.pair_scr[part, pl.ds(0, 2 * tiles)] = low
            self.pair_scr[part, pl.ds(2 * tiles, 2 * tiles)] = high
            self.float_scr[part, pl.ds(0, 2 * tiles)] = low.astype(jnp.float32)
            self.float_scr[part, pl.ds(2 * tiles, 2 * tiles)] = high.astype(jnp.float32)

    def fill(self, part, tables):
        directions, tiles, first = self.directions, self.tiles, self.first
        x_ref, pair_scr, float_scr = self.x_ref, self.pair_scr, self.float_scr
        stripes = self.stations // LANE
        depth = 6 * directions
        wide = (LANE // 16, 16, LANE)
        labels = lax.broadcasted_iota(jnp.int32, (LANE, LANE), 0).astype(jnp.float32)
        labels = labels.astype(jnp.bfloat16).reshape(wide)
        one, zero = jnp.ones(wide, jnp.bfloat16), jnp.zeros(wide, jnp.bfloat16)

        blank = jnp.zeros((16, LANE), jnp.bfloat16)

        def rows16(at):
            row = float_scr[part, pl.ds(at, 1)]
            return jnp.broadcast_to(row, (16, LANE)).astype(jnp.bfloat16)

        lefts, rights = [], []
        for tile in range(tiles):
            gains = []
            masks = []
            for side in range(2):
                low = pair_scr[part, pl.ds(side * tiles + tile, 1)]
                high = pair_scr[part, pl.ds((2 + side) * tiles + tile, 1)]
                low8 = jnp.broadcast_to(low, (directions, LANE))
                high8 = jnp.broadcast_to(high, (directions, LANE))
                highs = [high8 == s for s in range(stripes)]
                gains.append([pick(tables[j], low8, highs) for j in range(2)])
                high16 = rows16((2 + side) * tiles + tile)
                masks.append([high16 == jnp.bfloat16(s) for s in range(stripes)])
                hot = jnp.where(labels == rows16(side * tiles + tile)[None], one, zero)
                rights.append(hot.reshape(LANE, LANE))
            (gp_re, gp_im), (gq_re, gq_im) = gains
            coh_re, coh_im = [
                x_ref[part, pl.ds((2 * tile + j) * directions, directions)] for j in range(2)
            ]
            cross_re = gp_re * gq_re + gp_im * gq_im
            cross_im = gp_im * gq_re - gp_re * gq_im
            model_re = coh_re * cross_re - coh_im * cross_im
            model_im = coh_re * cross_im + coh_im * cross_re
            res_re = x_ref[part, pl.ds(first + tile, 1)] - jnp.sum(model_re, axis=0, keepdims=True)
            res_im = x_ref[part, pl.ds(first + tiles + tile, 1)] - jnp.sum(
                model_im, axis=0, keepdims=True
            )
            turn_re = coh_re * res_re + coh_im * res_im
            turn_im = coh_re * res_im - coh_im * res_re
            power = coh_re * coh_re + coh_im * coh_im
            terms_p = split_pack(
                turn_re * gq_re - turn_im * gq_im,
                turn_re * gq_im + turn_im * gq_re,
                power * (gq_re * gq_re + gq_im * gq_im),
            )
            terms_q = split_pack(
                turn_re * gp_re + turn_im * gp_im,
                turn_re * gp_im - turn_im * gp_re,
                power * (gp_re * gp_re + gp_im * gp_im),
            )
            for side, terms in enumerate((terms_p, terms_q)):
                lefts.append(
                    jnp.concatenate(
                        [
                            jnp.where(masks[side][s], term, blank)
                            for s in range(stripes)
                            for term in terms
                        ],
                        axis=0,
                    )
                )
            if (tile + 1) % GROUP == 0:
                self.sums_scr[...] += lax.dot_general(
                    jnp.concatenate(lefts, axis=1),
                    jnp.concatenate(rights, axis=1),
                    (((1,), (1,)), ((), ())),
                    preferred_element_type=jnp.float32,
                )
                lefts, rights = [], []

    def run(self, tables):
        @pl.loop(0, self.parts // UNROLL)
        def _(step):
            for i in range(UNROLL):
                self.fill(UNROLL * step + i, tables)


def read_tables(table_scr, stations):
    return [
        [table_scr[j, :, pl.ds(s * LANE, LANE)] for s in range(stations // LANE)]
        for j in range(2)
    ]


def own_rows(x_ref, at, owned, parts, directions):
    own = [x_ref[part, pl.ds(at, 2 * directions)] for part in range(parts)]
    return [
        jnp.concatenate([block[:, i * owned : (i + 1) * owned] for block in own], axis=1)
        for i in range(3)
    ]


def main_kernel(
    dims, owned, groups, penalty_ref, x_ref, out_ref, table_scr, base_scr, pair_scr, float_scr,
    sums_scr
):
    directions, tiles, stations, parts = dims
    stripes = stations // LANE
    depth = 6 * directions
    rho = per_direction(penalty_ref, (directions, 1), 1)
    mu = 0.5 * rho

    gain, cons, dual = own_rows(x_ref, tiles * (2 * directions + 4), owned, parts, directions)
    for j in range(2):
        cut = slice(j * directions, (j + 1) * directions)
        table_scr[j] = gain[cut]
        base_scr[j] = mu * cons[cut] - 0.5 * dual[cut]
        base_scr[2 + j] = dual[cut] / rho
    sweep = Sweep(dims, x_ref, pair_scr, float_scr, sums_scr)
    sweep.index()

    for gain_pass in range(PASSES):
        tables = read_tables(table_scr, stations)
        sums_scr[...] = jnp.zeros_like(sums_scr)
        sweep.run(tables)
        for s in range(stripes):
            cut = pl.ds(s * LANE, LANE)
            block = sums_scr[pl.ds(s * depth, depth)]
            total = block[0 : 2 * directions] + block[2 * directions : 4 * directions]
            power = block[4 * directions : 5 * directions] + block[5 * directions :]
            for j in range(2):
                top = total[j * directions : (j + 1) * directions]
                top = top + table_scr[j, :, cut] * power + base_scr[j, :, cut]
                table_scr[j, :, cut] = top / (power + mu)

    half = directions // 2
    for part in range(parts):
        cut = pl.ds(part * owned, owned)
        pieces = []
        for j in range(2):
            target = table_scr[j, :, cut] + base_scr[2 + j, :, cut]
            pieces += [target[0:half], target[half:]]
        block = jnp.concatenate(pieces, axis=1)
        for group in range(groups):
            out_ref[group * parts + part] = block


def finish_kernel(
    dims, penalty_ref, basis_ref, x_ref, dual_ref, gain_out, cons_out, dual_out, out_scr
):
    directions, chans, owned, count = dims
    half = directions // 2
    start = lax.axis_index("chan") * chans
    coefs = [jnp.zeros((half, LANE), jnp.float32) for _ in range(POLY)]
    for channel in range(count):
        block = x_ref[channel]
        for m in range(POLY):
            coefs[m] = coefs[m] + block * basis_ref[channel * POLY + m]
    for chan in range(chans):
        block = x_ref[start + chan]
        cons = coefs[0] * basis_ref[(start + chan) * POLY]
        for m in range(1, POLY):
            cons = cons + coefs[m] * basis_ref[(start + chan) * POLY + m]
        for j in range(2):
            rows = pl.ds(j * directions * chans + chan, directions, stride=chans)
            pieces = []
            for source in (block, cons):
                cuts = [source[:, (2 * j + h) * owned : (2 * j + h + 1) * owned] for h in range(2)]
                pieces.append(jnp.concatenate(cuts, axis=0))
            out_scr[rows, :] = jnp.concatenate(pieces + pieces, axis=1)
    whole = out_scr[...]
    rho = per_direction(penalty_ref, (2 * directions * chans, 1), chans)
    dual = dual_ref[...]
    gain = whole[:, 0:owned] - dual / rho
    cons = whole[:, owned : 2 * owned]
    gain_out[...] = gain
    cons_out[...] = cons
    dual_out[...] = dual + rho * (gain - cons)


def local(
    visibilities, coherencies, station_pairs, gains_start, consensus_prev, dual_prev, penalty
):
    owned, _, directions, chans = gains_start.shape
    lanes = visibilities.shape[2]
    parts = lax.axis_size("bl")
    groups = lax.axis_size("chan")
    stations = owned * parts
    tiles = lanes // LANE
    rows = directions * chans
    width = 2 * rows
    depth = 6 * directions * (stations // LANE)

    def flat(array):
        return jnp.transpose(array, (1, 2, 3, 0)).reshape(width, owned)

    def call(kernel, shapes, specs, limit=LIMIT, **extra):
        return pl.pallas_call(
            kernel,
            out_shape=[jax.ShapeDtypeStruct(s, jnp.float32) for s in shapes],
            in_specs=specs,
            out_specs=[VMEM] * len(shapes),
            compiler_params=limit,
            **extra,
        )

    own = (flat(gains_start), flat(consensus_prev), flat(dual_prev))
    basis = jnp.asarray(poly_basis(chans * groups, POLY).reshape(-1))

    count = tiles * (2 * directions + 4) + 2 * directions
    packed = pl.pallas_call(
        functools.partial(prep_kernel, (directions, chans, tiles, owned)),
        out_shape=jax.ShapeDtypeStruct((chans, count, LANE), jnp.float32),
        in_specs=[HBM] * 6,
        out_specs=HBM,
        scratch_shapes=[
            pltpu.VMEM((tiles, width, LANE), jnp.float32),
            pltpu.VMEM((2, tiles * chans, LANE), jnp.float32),
            pltpu.VMEM(station_pairs.shape, jnp.int32),
            pltpu.VMEM((3, width, owned), jnp.float32),
            pltpu.VMEM((width, LANE), jnp.float32),
            pltpu.VMEM((chans, count, LANE), jnp.float32),
            pltpu.SemaphoreType.DMA((2 * tiles + 4,)),
            pltpu.SemaphoreType.DMA((tiles // 2 + 1,)),
        ],
    )(visibilities, coherencies.reshape(width, lanes), station_pairs, *own)
    x = lax.all_to_all(packed, "bl", 0, 0, tiled=True)
    dims = (directions, tiles, stations, parts)
    (sent,) = call(
        functools.partial(main_kernel, dims, owned, groups),
        [(groups * parts, directions // 2, LANE)],
        [SMEM, VMEM],
        scratch_shapes=[
            pltpu.VMEM((2, directions, stations), jnp.float32),
            pltpu.VMEM((4, directions, stations), jnp.float32),
            pltpu.VMEM((parts, 4 * tiles, LANE), jnp.int32),
            pltpu.VMEM((parts, 4 * tiles, LANE), jnp.float32),
            pltpu.VMEM((depth, LANE), jnp.float32),
        ],
    )(penalty, x)
    held = lax.all_to_all(sent, ("chan", "bl"), 0, 0, tiled=True)
    outs = call(
        functools.partial(finish_kernel, (directions, chans, owned, chans * groups)),
        [(width, owned)] * 3,
        [SMEM, SMEM, VMEM, VMEM],
        scratch_shapes=[pltpu.VMEM((width, LANE), jnp.float32)],
    )(penalty, basis, held, own[2])

    def back(array):
        return jnp.transpose(array.reshape(2, directions, chans, owned), (3, 0, 1, 2))

    return tuple(back(array) for array in outs)


def solution(mesh):
    placed = (
        P(None, "chan", "bl"),
        P(None, None, "chan", "bl"),
        P(None, "bl"),
        P("bl", None, None, "chan"),
        P("bl", None, None, "chan"),
        P("bl", None, None, "chan"),
        P(),
    )
    return jax.shard_map(
        local,
        mesh=mesh,
        in_specs=placed,
        out_specs=(
            P("bl", None, None, "chan"),
            P("bl", None, None, "chan"),
            P("bl", None, None, "chan"),
        ),
        check_vma=False,
    )
```

```python
import functools

import jax
import jax.numpy as jnp
import numpy as np
from jax import lax
from jax.experimental import pallas as pl
from jax.experimental.pallas import tpu as pltpu
from jax.sharding import PartitionSpec as P

PASSES = 2
POLY = 4
LANE = 128
GROUP = 1
UNROLL = 8
VMEM = pl.BlockSpec(memory_space=pltpu.VMEM)
SMEM = pl.BlockSpec(memory_space=pltpu.SMEM)
HBM = pl.BlockSpec(memory_space=pltpu.HBM)
LIMIT = pltpu.CompilerParams(vmem_limit_bytes=40 * 1024 * 1024)


def poly_basis(count, order):
    freq = 2.0 * (np.arange(count).astype(np.float64) + 0.5) / count - 1.0
    columns = []
    for power in range(order):
        vector = freq**power
        for before in columns:
            vector = vector - np.sum(before * vector) * before
        columns.append(vector / np.sqrt(np.sum(vector * vector)))
    return np.stack(columns, axis=1).astype(np.float32)


def prep_kernel(
    dims,
    vis_hbm,
    coh_hbm,
    pairs_hbm,
    gain_hbm,
    cons_hbm,
    dual_hbm,
    out_hbm,
    coh_scr,
    vis_scr,
    vis_raw,
    pairs_scr,
    own_scr,
    all_scr,
    out_scr,
    sems,
    out_sems,
):
    directions, chans, tiles, owned = dims
    depth = 2 * directions
    base = tiles * depth
    copies = [pltpu.make_async_copy(pairs_hbm, pairs_scr, sems.at[tiles])]
    for i, ref in enumerate((gain_hbm, cons_hbm, dual_hbm)):
        copies.append(pltpu.make_async_copy(ref, own_scr.at[i], sems.at[tiles + 1 + i]))
    coh_copies = []
    for tile in range(tiles):
        cut = pl.ds(tile * LANE, LANE)
        coh_copies.append(
            pltpu.make_async_copy(coh_hbm.at[:, cut], coh_scr.at[tile], sems.at[tile])
        )
    vis_copy = pltpu.make_async_copy(vis_hbm, vis_raw, sems.at[tiles + 4])
    for copy in copies + coh_copies + [vis_copy]:
        copy.start()
    for copy in copies:
        copy.wait()
    own = [own_scr[i] for i in range(3)]
    all_scr[...] = jnp.concatenate(own + [jnp.zeros_like(own[0])], axis=1)
    for chan in range(chans):
        rows = pl.ds(chan, depth, stride=chans)
        out_scr[chan, pl.ds(base + 4 * tiles, depth)] = all_scr[rows, :]
    for side in range(2):
        for tile in range(tiles):
            row = pairs_scr[side : side + 1, pl.ds(tile * LANE, LANE)].astype(jnp.float32)
            all_scr[pl.ds(side * tiles + tile, 1), :] = row
    pairs = all_scr[pl.ds(0, 2 * tiles)]
    for chan in range(chans):
        out_scr[chan, pl.ds(base + 2 * tiles, 2 * tiles)] = pairs
    out_copies = []

    def send(first, rows):
        cut = pl.ds(first, rows)
        copy = pltpu.make_async_copy(
            out_scr.at[:, cut], out_hbm.at[:, cut], out_sems.at[len(out_copies)]
        )
        copy.start()
        out_copies.append(copy)

    for tile in range(tiles):
        coh_copies[tile].wait()
        for chan in range(chans):
            for part in range(2):
                out_scr[chan, pl.ds((2 * tile + part) * directions, directions)] = coh_scr[
                    tile, pl.ds(part * directions * chans + chan, directions, stride=chans)
                ]
        if tile % 4 == 3:
            send((tile - 3) * depth, 4 * depth)
    vis_copy.wait()
    for tile in range(tiles):
        for part in range(2):
            vis_scr[part, pl.ds(tile * chans, chans)] = vis_raw[part, :, pl.ds(tile * LANE, LANE)]
    for chan in range(chans):
        for part in range(2):
            out_scr[chan, pl.ds(base + part * tiles, tiles)] = vis_scr[
                part, pl.ds(chan, tiles, stride=chans)
            ]
    send(base, 4 * tiles + depth)
    for copy in out_copies:
        copy.wait()


def pick(tables, low, highs):
    out = None
    for index, table in enumerate(tables):
        found = jnp.take_along_axis(table, low, axis=1)
        out = found if index == 0 else jnp.where(highs[index], found, out)
    return out


def split_pack(re, im, power):
    pair = jnp.concatenate([re, im], axis=0)
    upper = pair.astype(jnp.bfloat16)
    lower = (pair - upper.astype(jnp.float32)).astype(jnp.bfloat16)
    rest = power - power.astype(jnp.bfloat16).astype(jnp.float32)
    last = jnp.concatenate([power, rest], axis=0).astype(jnp.bfloat16)
    return upper, lower, last


def per_direction(penalty_ref, shape, period):
    row = (lax.broadcasted_iota(jnp.int32, shape, 0) // period) % penalty_ref.shape[0]
    rho = jnp.zeros(shape, jnp.float32)
    for k in range(penalty_ref.shape[0]):
        rho = jnp.where(row == k, penalty_ref[k], rho)
    return rho


class Sweep:
    def __init__(self, dims, x_ref, pair_scr, float_scr, sums_scr):
        self.directions, self.tiles, self.stations, self.parts = dims
        self.x_ref, self.sums_scr = x_ref, sums_scr
        self.pair_scr, self.float_scr = pair_scr, float_scr
        self.first = self.tiles * 2 * self.directions

    def index(self):
        tiles = self.tiles
        for part in range(self.parts):
            whole = self.x_ref[part, pl.ds(self.first + 2 * tiles, 2 * tiles)].astype(jnp.int32)
            low, high = jnp.bitwise_and(whole, LANE - 1), jnp.right_shift(whole, 7)
            self.pair_scr[part, pl.ds(0, 2 * tiles)] = low
            self.pair_scr[part, pl.ds(2 * tiles, 2 * tiles)] = high
            self.float_scr[part, pl.ds(0, 2 * tiles)] = low.astype(jnp.float32)
            self.float_scr[part, pl.ds(2 * tiles, 2 * tiles)] = high.astype(jnp.float32)

    def fill(self, part, tables):
        directions, tiles, first = self.directions, self.tiles, self.first
        x_ref, pair_scr, float_scr = self.x_ref, self.pair_scr, self.float_scr
        stripes = self.stations // LANE
        depth = 6 * directions
        wide = (LANE // 16, 16, LANE)
        labels = lax.broadcasted_iota(jnp.int32, (LANE, LANE), 0).astype(jnp.float32)
        labels = labels.astype(jnp.bfloat16).reshape(wide)
        one, zero = jnp.ones(wide, jnp.bfloat16), jnp.zeros(wide, jnp.bfloat16)

        blank = jnp.zeros((16, LANE), jnp.bfloat16)

        def rows16(at):
            row = float_scr[part, pl.ds(at, 1)]
            return jnp.broadcast_to(row, (16, LANE)).astype(jnp.bfloat16)

        lefts, rights = [], []
        for tile in range(tiles):
            gains = []
            masks = []
            for side in range(2):
                low = pair_scr[part, pl.ds(side * tiles + tile, 1)]
                high = pair_scr[part, pl.ds((2 + side) * tiles + tile, 1)]
                low8 = jnp.broadcast_to(low, (directions, LANE))
                high8 = jnp.broadcast_to(high, (directions, LANE))
                highs = [high8 == s for s in range(stripes)]
                gains.append([pick(tables[j], low8, highs) for j in range(2)])
                high16 = rows16((2 + side) * tiles + tile)
                masks.append([high16 == jnp.bfloat16(s) for s in range(stripes)])
                hot = jnp.where(labels == rows16(side * tiles + tile)[None], one, zero)
                rights.append(hot.reshape(LANE, LANE))
            (gp_re, gp_im), (gq_re, gq_im) = gains
            coh_re, coh_im = [
                x_ref[part, pl.ds((2 * tile + j) * directions, directions)] for j in range(2)
            ]
            cross_re = gp_re * gq_re + gp_im * gq_im
            cross_im = gp_im * gq_re - gp_re * gq_im
            model_re = coh_re * cross_re - coh_im * cross_im
            model_im = coh_re * cross_im + coh_im * cross_re
            res_re = x_ref[part, pl.ds(first + tile, 1)] - jnp.sum(model_re, axis=0, keepdims=True)
            res_im = x_ref[part, pl.ds(first + tiles + tile, 1)] - jnp.sum(
                model_im, axis=0, keepdims=True
            )
            turn_re = coh_re * res_re + coh_im * res_im
            turn_im = coh_re * res_im - coh_im * res_re
            power = coh_re * coh_re + coh_im * coh_im
            terms_p = split_pack(
                turn_re * gq_re - turn_im * gq_im,
                turn_re * gq_im + turn_im * gq_re,
                power * (gq_re * gq_re + gq_im * gq_im),
            )
            terms_q = split_pack(
                turn_re * gp_re + turn_im * gp_im,
                turn_re * gp_im - turn_im * gp_re,
                power * (gp_re * gp_re + gp_im * gp_im),
            )
            for side, terms in enumerate((terms_p, terms_q)):
                lefts.append(
                    jnp.concatenate(
                        [
                            jnp.where(masks[side][s], term, blank)
                            for s in range(stripes)
                            for term in terms
                        ],
                        axis=0,
                    )
                )
            if (tile + 1) % GROUP == 0:
                self.sums_scr[...] += lax.dot_general(
                    jnp.concatenate(lefts, axis=1),
                    jnp.concatenate(rights, axis=1),
                    (((1,), (1,)), ((), ())),
                    preferred_element_type=jnp.float32,
                )
                lefts, rights = [], []

    def run(self, tables):
        @pl.loop(0, self.parts // UNROLL)
        def _(step):
            for i in range(UNROLL):
                self.fill(UNROLL * step + i, tables)


def read_tables(table_scr, stations):
    return [
        [table_scr[j, :, pl.ds(s * LANE, LANE)] for s in range(stations // LANE)]
        for j in range(2)
    ]


def own_rows(x_ref, at, owned, parts, directions):
    own = [x_ref[part, pl.ds(at, 2 * directions)] for part in range(parts)]
    return [
        jnp.concatenate([block[:, i * owned : (i + 1) * owned] for block in own], axis=1)
        for i in range(3)
    ]


def main_kernel(
    dims, owned, groups, penalty_ref, x_ref, out_ref, table_scr, base_scr, pair_scr, float_scr,
    sums_scr
):
    directions, tiles, stations, parts = dims
    stripes = stations // LANE
    depth = 6 * directions
    rho = per_direction(penalty_ref, (directions, 1), 1)
    mu = 0.5 * rho

    gain, cons, dual = own_rows(x_ref, tiles * (2 * directions + 4), owned, parts, directions)
    for j in range(2):
        cut = slice(j * directions, (j + 1) * directions)
        table_scr[j] = gain[cut]
        base_scr[j] = mu * cons[cut] - 0.5 * dual[cut]
        base_scr[2 + j] = dual[cut] / rho
    sweep = Sweep(dims, x_ref, pair_scr, float_scr, sums_scr)
    sweep.index()

    for gain_pass in range(PASSES):
        tables = read_tables(table_scr, stations)
        sums_scr[...] = jnp.zeros_like(sums_scr)
        sweep.run(tables)
        for s in range(stripes):
            cut = pl.ds(s * LANE, LANE)
            block = sums_scr[pl.ds(s * depth, depth)]
            total = block[0 : 2 * directions] + block[2 * directions : 4 * directions]
            power = block[4 * directions : 5 * directions] + block[5 * directions :]
            for j in range(2):
                top = total[j * directions : (j + 1) * directions]
                top = top + table_scr[j, :, cut] * power + base_scr[j, :, cut]
                table_scr[j, :, cut] = top / (power + mu)

    half = directions // 2
    for part in range(parts):
        cut = pl.ds(part * owned, owned)
        pieces = []
        for j in range(2):
            target = table_scr[j, :, cut] + base_scr[2 + j, :, cut]
            pieces += [target[0:half], target[half:]]
        block = jnp.concatenate(pieces, axis=1)
        for group in range(groups):
            out_ref[group * parts + part] = block


def finish_kernel(
    dims, penalty_ref, basis_ref, x_ref, dual_ref, gain_out, cons_out, dual_out, out_scr
):
    directions, chans, owned, count = dims
    half = directions // 2
    start = lax.axis_index("chan") * chans
    chains = [[jnp.zeros((half, LANE), jnp.float32)] * 4 for _ in range(POLY)]
    for channel in range(count):
        block = x_ref[channel]
        for m in range(POLY):
            chains[m][channel % 4] += block * basis_ref[channel * POLY + m]
    coefs = [(c[0] + c[1]) + (c[2] + c[3]) for c in chains]
    for chan in range(chans):
        block = x_ref[start + chan]
        cons = coefs[0] * basis_ref[(start + chan) * POLY]
        for m in range(1, POLY):
            cons = cons + coefs[m] * basis_ref[(start + chan) * POLY + m]
        for j in range(2):
            rows = pl.ds(j * directions * chans + chan, directions, stride=chans)
            pieces = []
            for source in (block, cons):
                cuts = [source[:, (2 * j + h) * owned : (2 * j + h + 1) * owned] for h in range(2)]
                pieces.append(jnp.concatenate(cuts, axis=0))
            out_scr[rows, :] = jnp.concatenate(pieces + pieces, axis=1)
    whole = out_scr[...]
    rho = per_direction(penalty_ref, (2 * directions * chans, 1), chans)
    dual = dual_ref[...]
    gain = whole[:, 0:owned] - dual / rho
    cons = whole[:, owned : 2 * owned]
    gain_out[...] = gain
    cons_out[...] = cons
    dual_out[...] = dual + rho * (gain - cons)


def local(
    visibilities, coherencies, station_pairs, gains_start, consensus_prev, dual_prev, penalty
):
    owned, _, directions, chans = gains_start.shape
    lanes = visibilities.shape[2]
    parts = lax.axis_size("bl")
    groups = lax.axis_size("chan")
    stations = owned * parts
    tiles = lanes // LANE
    rows = directions * chans
    width = 2 * rows
    depth = 6 * directions * (stations // LANE)

    def flat(array):
        return jnp.transpose(array, (1, 2, 3, 0)).reshape(width, owned)

    def call(kernel, shapes, specs, limit=LIMIT, **extra):
        return pl.pallas_call(
            kernel,
            out_shape=[jax.ShapeDtypeStruct(s, jnp.float32) for s in shapes],
            in_specs=specs,
            out_specs=[VMEM] * len(shapes),
            compiler_params=limit,
            **extra,
        )

    own = (flat(gains_start), flat(consensus_prev), flat(dual_prev))
    basis = jnp.asarray(poly_basis(chans * groups, POLY).reshape(-1))

    count = tiles * (2 * directions + 4) + 2 * directions
    packed = pl.pallas_call(
        functools.partial(prep_kernel, (directions, chans, tiles, owned)),
        out_shape=jax.ShapeDtypeStruct((chans, count, LANE), jnp.float32),
        in_specs=[HBM] * 6,
        out_specs=HBM,
        scratch_shapes=[
            pltpu.VMEM((tiles, width, LANE), jnp.float32),
            pltpu.VMEM((2, tiles * chans, LANE), jnp.float32),
            pltpu.VMEM(visibilities.shape, jnp.float32),
            pltpu.VMEM(station_pairs.shape, jnp.int32),
            pltpu.VMEM((3, width, owned), jnp.float32),
            pltpu.VMEM((width, LANE), jnp.float32),
            pltpu.VMEM((chans, count, LANE), jnp.float32),
            pltpu.SemaphoreType.DMA((tiles + 5,)),
            pltpu.SemaphoreType.DMA((tiles // 4 + 1,)),
        ],
    )(visibilities, coherencies.reshape(width, lanes), station_pairs, *own)
    x = lax.all_to_all(packed, "bl", 0, 0, tiled=True)
    dims = (directions, tiles, stations, parts)
    (sent,) = call(
        functools.partial(main_kernel, dims, owned, groups),
        [(groups * parts, directions // 2, LANE)],
        [SMEM, VMEM],
        scratch_shapes=[
            pltpu.VMEM((2, directions, stations), jnp.float32),
            pltpu.VMEM((4, directions, stations), jnp.float32),
            pltpu.VMEM((parts, 4 * tiles, LANE), jnp.int32),
            pltpu.VMEM((parts, 4 * tiles, LANE), jnp.float32),
            pltpu.VMEM((depth, LANE), jnp.float32),
        ],
    )(penalty, x)
    held = lax.all_to_all(sent, ("chan", "bl"), 0, 0, tiled=True)
    outs = call(
        functools.partial(finish_kernel, (directions, chans, owned, chans * groups)),
        [(width, owned)] * 3,
        [SMEM, SMEM, VMEM, VMEM],
        scratch_shapes=[pltpu.VMEM((width, LANE), jnp.float32)],
    )(penalty, basis, held, own[2])

    def back(array):
        return jnp.transpose(array.reshape(2, directions, chans, owned), (3, 0, 1, 2))

    return tuple(back(array) for array in outs)


def solution(mesh):
    placed = (
        P(None, "chan", "bl"),
        P(None, None, "chan", "bl"),
        P(None, "bl"),
        P("bl", None, None, "chan"),
        P("bl", None, None, "chan"),
        P("bl", None, None, "chan"),
        P(),
    )
    return jax.shard_map(
        local,
        mesh=mesh,
        in_specs=placed,
        out_specs=(
            P("bl", None, None, "chan"),
            P("bl", None, None, "chan"),
            P("bl", None, None, "chan"),
        ),
        check_vma=False,
    )
```

```python
import functools

import jax
import jax.numpy as jnp
import numpy as np
from jax import lax
from jax.experimental import pallas as pl
from jax.experimental.pallas import tpu as pltpu
from jax.sharding import PartitionSpec as P

PASSES = 2
POLY = 4
LANE = 128
GROUP = 1
UNROLL = 8
VMEM = pl.BlockSpec(memory_space=pltpu.VMEM)
SMEM = pl.BlockSpec(memory_space=pltpu.SMEM)
HBM = pl.BlockSpec(memory_space=pltpu.HBM)
LIMIT = pltpu.CompilerParams(vmem_limit_bytes=40 * 1024 * 1024)


def poly_basis(count, order):
    freq = 2.0 * (np.arange(count).astype(np.float64) + 0.5) / count - 1.0
    columns = []
    for power in range(order):
        vector = freq**power
        for before in columns:
            vector = vector - np.sum(before * vector) * before
        columns.append(vector / np.sqrt(np.sum(vector * vector)))
    return np.stack(columns, axis=1).astype(np.float32)


def prep_kernel(
    dims,
    vis_hbm,
    coh_hbm,
    pairs_hbm,
    gain_hbm,
    cons_hbm,
    dual_hbm,
    out_hbm,
    coh_scr,
    vis_scr,
    vis_raw,
    pairs_scr,
    own_scr,
    all_scr,
    out_scr,
    sems,
    out_sems,
):
    directions, chans, tiles, owned = dims
    depth = 2 * directions
    base = tiles * depth
    copies = [pltpu.make_async_copy(pairs_hbm, pairs_scr, sems.at[tiles])]
    for i, ref in enumerate((gain_hbm, cons_hbm, dual_hbm)):
        copies.append(pltpu.make_async_copy(ref, own_scr.at[i], sems.at[tiles + 1 + i]))
    coh_copies = []
    for tile in range(tiles):
        cut = pl.ds(tile * LANE, LANE)
        coh_copies.append(
            pltpu.make_async_copy(coh_hbm.at[:, cut], coh_scr.at[tile], sems.at[tile])
        )
    vis_copy = pltpu.make_async_copy(vis_hbm, vis_raw, sems.at[tiles + 4])
    for copy in copies + [vis_copy] + coh_copies:
        copy.start()
    for copy in copies:
        copy.wait()
    own = [own_scr[i] for i in range(3)]
    all_scr[...] = jnp.concatenate(own + [jnp.zeros_like(own[0])], axis=1)
    for chan in range(chans):
        rows = pl.ds(chan, depth, stride=chans)
        out_scr[chan, pl.ds(base + 4 * tiles, depth)] = all_scr[rows, :]
    for side in range(2):
        for tile in range(tiles):
            row = pairs_scr[side : side + 1, pl.ds(tile * LANE, LANE)].astype(jnp.float32)
            all_scr[pl.ds(side * tiles + tile, 1), :] = row
    pairs = all_scr[pl.ds(0, 2 * tiles)]
    for chan in range(chans):
        out_scr[chan, pl.ds(base + 2 * tiles, 2 * tiles)] = pairs
    out_copies = []

    def send(first, rows):
        cut = pl.ds(first, rows)
        copy = pltpu.make_async_copy(
            out_scr.at[:, cut], out_hbm.at[:, cut], out_sems.at[len(out_copies)]
        )
        copy.start()
        out_copies.append(copy)

    vis_copy.wait()
    for tile in range(tiles):
        for part in range(2):
            vis_scr[part, pl.ds(tile * chans, chans)] = vis_raw[part, :, pl.ds(tile * LANE, LANE)]
    for chan in range(chans):
        for part in range(2):
            out_scr[chan, pl.ds(base + part * tiles, tiles)] = vis_scr[
                part, pl.ds(chan, tiles, stride=chans)
            ]
    send(base, 4 * tiles + depth)
    for tile in range(tiles):
        coh_copies[tile].wait()
        for chan in range(chans):
            for part in range(2):
                out_scr[chan, pl.ds((2 * tile + part) * directions, directions)] = coh_scr[
                    tile, pl.ds(part * directions * chans + chan, directions, stride=chans)
                ]
        if tile % 4 == 3:
            send((tile - 3) * depth, 4 * depth)
    for copy in out_copies:
        copy.wait()


def pick(tables, low, highs):
    out = None
    for index, table in enumerate(tables):
        found = jnp.take_along_axis(table, low, axis=1)
        out = found if index == 0 else jnp.where(highs[index], found, out)
    return out


def split_pack(re, im, power):
    pair = jnp.concatenate([re, im], axis=0)
    upper = pair.astype(jnp.bfloat16)
    lower = (pair - upper.astype(jnp.float32)).astype(jnp.bfloat16)
    rest = power - power.astype(jnp.bfloat16).astype(jnp.float32)
    last = jnp.concatenate([power, rest], axis=0).astype(jnp.bfloat16)
    return upper, lower, last


def per_direction(penalty_ref, shape, period):
    row = (lax.broadcasted_iota(jnp.int32, shape, 0) // period) % penalty_ref.shape[0]
    rho = jnp.zeros(shape, jnp.float32)
    for k in range(penalty_ref.shape[0]):
        rho = jnp.where(row == k, penalty_ref[k], rho)
    return rho


class Sweep:
    def __init__(self, dims, x_ref, pair_scr, float_scr, sums_scr):
        self.directions, self.tiles, self.stations, self.parts = dims
        self.x_ref, self.sums_scr = x_ref, sums_scr
        self.pair_scr, self.float_scr = pair_scr, float_scr
        self.first = self.tiles * 2 * self.directions

    def index(self):
        tiles = self.tiles
        for part in range(self.parts):
            whole = self.x_ref[part, pl.ds(self.first + 2 * tiles, 2 * tiles)].astype(jnp.int32)
            low, high = jnp.bitwise_and(whole, LANE - 1), jnp.right_shift(whole, 7)
            self.pair_scr[part, pl.ds(0, 2 * tiles)] = low
            self.pair_scr[part, pl.ds(2 * tiles, 2 * tiles)] = high
            self.float_scr[part, pl.ds(0, 2 * tiles)] = low.astype(jnp.float32)
            self.float_scr[part, pl.ds(2 * tiles, 2 * tiles)] = high.astype(jnp.float32)

    def fill(self, part, tables):
        directions, tiles, first = self.directions, self.tiles, self.first
        x_ref, pair_scr, float_scr = self.x_ref, self.pair_scr, self.float_scr
        stripes = self.stations // LANE
        depth = 6 * directions
        wide = (LANE // 16, 16, LANE)
        labels = lax.broadcasted_iota(jnp.int32, (LANE, LANE), 0).astype(jnp.float32)
        labels = labels.astype(jnp.bfloat16).reshape(wide)
        one, zero = jnp.ones(wide, jnp.bfloat16), jnp.zeros(wide, jnp.bfloat16)

        blank = jnp.zeros((16, LANE), jnp.bfloat16)

        def rows16(at):
            row = float_scr[part, pl.ds(at, 1)]
            return jnp.broadcast_to(row, (16, LANE)).astype(jnp.bfloat16)

        lefts, rights = [], []
        for tile in range(tiles):
            gains = []
            masks = []
            for side in range(2):
                low = pair_scr[part, pl.ds(side * tiles + tile, 1)]
                high = pair_scr[part, pl.ds((2 + side) * tiles + tile, 1)]
                low8 = jnp.broadcast_to(low, (directions, LANE))
                high8 = jnp.broadcast_to(high, (directions, LANE))
                highs = [high8 == s for s in range(stripes)]
                gains.append([pick(tables[j], low8, highs) for j in range(2)])
                high16 = rows16((2 + side) * tiles + tile)
                masks.append([high16 == jnp.bfloat16(s) for s in range(stripes)])
                hot = jnp.where(labels == rows16(side * tiles + tile)[None], one, zero)
                rights.append(hot.reshape(LANE, LANE))
            (gp_re, gp_im), (gq_re, gq_im) = gains
            coh_re, coh_im = [
                x_ref[part, pl.ds((2 * tile + j) * directions, directions)] for j in range(2)
            ]
            cross_re = gp_re * gq_re + gp_im * gq_im
            cross_im = gp_im * gq_re - gp_re * gq_im
            model_re = coh_re * cross_re - coh_im * cross_im
            model_im = coh_re * cross_im + coh_im * cross_re
            res_re = x_ref[part, pl.ds(first + tile, 1)] - jnp.sum(model_re, axis=0, keepdims=True)
            res_im = x_ref[part, pl.ds(first + tiles + tile, 1)] - jnp.sum(
                model_im, axis=0, keepdims=True
            )
            turn_re = coh_re * res_re + coh_im * res_im
            turn_im = coh_re * res_im - coh_im * res_re
            power = coh_re * coh_re + coh_im * coh_im
            terms_p = split_pack(
                turn_re * gq_re - turn_im * gq_im,
                turn_re * gq_im + turn_im * gq_re,
                power * (gq_re * gq_re + gq_im * gq_im),
            )
            terms_q = split_pack(
                turn_re * gp_re + turn_im * gp_im,
                turn_re * gp_im - turn_im * gp_re,
                power * (gp_re * gp_re + gp_im * gp_im),
            )
            for side, terms in enumerate((terms_p, terms_q)):
                lefts.append(
                    jnp.concatenate(
                        [
                            jnp.where(masks[side][s], term, blank)
                            for s in range(stripes)
                            for term in terms
                        ],
                        axis=0,
                    )
                )
            if (tile + 1) % GROUP == 0:
                self.sums_scr[...] += lax.dot_general(
                    jnp.concatenate(lefts, axis=1),
                    jnp.concatenate(rights, axis=1),
                    (((1,), (1,)), ((), ())),
                    preferred_element_type=jnp.float32,
                )
                lefts, rights = [], []

    def run(self, tables):
        @pl.loop(0, self.parts // UNROLL)
        def _(step):
            for i in range(UNROLL):
                self.fill(UNROLL * step + i, tables)


def read_tables(table_scr, stations):
    return [
        [table_scr[j, :, pl.ds(s * LANE, LANE)] for s in range(stations // LANE)]
        for j in range(2)
    ]


def own_rows(x_ref, at, owned, parts, directions):
    own = [x_ref[part, pl.ds(at, 2 * directions)] for part in range(parts)]
    return [
        jnp.concatenate([block[:, i * owned : (i + 1) * owned] for block in own], axis=1)
        for i in range(3)
    ]


def main_kernel(
    dims, owned, groups, penalty_ref, x_ref, out_ref, table_scr, base_scr, pair_scr, float_scr,
    sums_scr
):
    directions, tiles, stations, parts = dims
    stripes = stations // LANE
    depth = 6 * directions
    rho = per_direction(penalty_ref, (directions, 1), 1)
    mu = 0.5 * rho

    gain, cons, dual = own_rows(x_ref, tiles * (2 * directions + 4), owned, parts, directions)
    for j in range(2):
        cut = slice(j * directions, (j + 1) * directions)
        table_scr[j] = gain[cut]
        base_scr[j] = mu * cons[cut] - 0.5 * dual[cut]
        base_scr[2 + j] = dual[cut] / rho
    sweep = Sweep(dims, x_ref, pair_scr, float_scr, sums_scr)
    sweep.index()

    for gain_pass in range(PASSES):
        tables = read_tables(table_scr, stations)
        sums_scr[...] = jnp.zeros_like(sums_scr)
        sweep.run(tables)
        for s in range(stripes):
            cut = pl.ds(s * LANE, LANE)
            block = sums_scr[pl.ds(s * depth, depth)]
            total = block[0 : 2 * directions] + block[2 * directions : 4 * directions]
            power = block[4 * directions : 5 * directions] + block[5 * directions :]
            for j in range(2):
                top = total[j * directions : (j + 1) * directions]
                top = top + table_scr[j, :, cut] * power + base_scr[j, :, cut]
                table_scr[j, :, cut] = top / (power + mu)

    half = directions // 2
    for part in range(parts):
        cut = pl.ds(part * owned, owned)
        pieces = []
        for j in range(2):
            target = table_scr[j, :, cut] + base_scr[2 + j, :, cut]
            pieces += [target[0:half], target[half:]]
        block = jnp.concatenate(pieces, axis=1)
        for group in range(groups):
            out_ref[group * parts + part] = block


def finish_kernel(
    dims, penalty_ref, basis_ref, x_ref, dual_ref, gain_out, cons_out, dual_out, out_scr
):
    directions, chans, owned, count = dims
    half = directions // 2
    start = lax.axis_index("chan") * chans
    chains = [[jnp.zeros((half, LANE), jnp.float32)] * 4 for _ in range(POLY)]
    for channel in range(count):
        block = x_ref[channel]
        for m in range(POLY):
            chains[m][channel % 4] += block * basis_ref[channel * POLY + m]
    coefs = [(c[0] + c[1]) + (c[2] + c[3]) for c in chains]
    for chan in range(chans):
        block = x_ref[start + chan]
        cons = coefs[0] * basis_ref[(start + chan) * POLY]
        for m in range(1, POLY):
            cons = cons + coefs[m] * basis_ref[(start + chan) * POLY + m]
        for j in range(2):
            rows = pl.ds(j * directions * chans + chan, directions, stride=chans)
            pieces = []
            for source in (block, cons):
                cuts = [source[:, (2 * j + h) * owned : (2 * j + h + 1) * owned] for h in range(2)]
                pieces.append(jnp.concatenate(cuts, axis=0))
            out_scr[rows, :] = jnp.concatenate(pieces + pieces, axis=1)
    whole = out_scr[...]
    rho = per_direction(penalty_ref, (2 * directions * chans, 1), chans)
    dual = dual_ref[...]
    gain = whole[:, 0:owned] - dual / rho
    cons = whole[:, owned : 2 * owned]
    gain_out[...] = gain
    cons_out[...] = cons
    dual_out[...] = dual + rho * (gain - cons)


def local(
    visibilities, coherencies, station_pairs, gains_start, consensus_prev, dual_prev, penalty
):
    owned, _, directions, chans = gains_start.shape
    lanes = visibilities.shape[2]
    parts = lax.axis_size("bl")
    groups = lax.axis_size("chan")
    stations = owned * parts
    tiles = lanes // LANE
    rows = directions * chans
    width = 2 * rows
    depth = 6 * directions * (stations // LANE)

    def flat(array):
        return jnp.transpose(array, (1, 2, 3, 0)).reshape(width, owned)

    def call(kernel, shapes, specs, limit=LIMIT, **extra):
        return pl.pallas_call(
            kernel,
            out_shape=[jax.ShapeDtypeStruct(s, jnp.float32) for s in shapes],
            in_specs=specs,
            out_specs=[VMEM] * len(shapes),
            compiler_params=limit,
            **extra,
        )

    own = (flat(gains_start), flat(consensus_prev), flat(dual_prev))
    basis = jnp.asarray(poly_basis(chans * groups, POLY).reshape(-1))

    count = tiles * (2 * directions + 4) + 2 * directions
    packed = pl.pallas_call(
        functools.partial(prep_kernel, (directions, chans, tiles, owned)),
        out_shape=jax.ShapeDtypeStruct((chans, count, LANE), jnp.float32),
        in_specs=[HBM] * 6,
        out_specs=HBM,
        scratch_shapes=[
            pltpu.VMEM((tiles, width, LANE), jnp.float32),
            pltpu.VMEM((2, tiles * chans, LANE), jnp.float32),
            pltpu.VMEM(visibilities.shape, jnp.float32),
            pltpu.VMEM(station_pairs.shape, jnp.int32),
            pltpu.VMEM((3, width, owned), jnp.float32),
            pltpu.VMEM((width, LANE), jnp.float32),
            pltpu.VMEM((chans, count, LANE), jnp.float32),
            pltpu.SemaphoreType.DMA((tiles + 5,)),
            pltpu.SemaphoreType.DMA((tiles // 4 + 1,)),
        ],
    )(visibilities, coherencies.reshape(width, lanes), station_pairs, *own)
    x = lax.all_to_all(packed, "bl", 0, 0, tiled=True)
    dims = (directions, tiles, stations, parts)
    (sent,) = call(
        functools.partial(main_kernel, dims, owned, groups),
        [(groups * parts, directions // 2, LANE)],
        [SMEM, VMEM],
        scratch_shapes=[
            pltpu.VMEM((2, directions, stations), jnp.float32),
            pltpu.VMEM((4, directions, stations), jnp.float32),
            pltpu.VMEM((parts, 4 * tiles, LANE), jnp.int32),
            pltpu.VMEM((parts, 4 * tiles, LANE), jnp.float32),
            pltpu.VMEM((depth, LANE), jnp.float32),
        ],
    )(penalty, x)
    held = lax.all_to_all(sent, ("chan", "bl"), 0, 0, tiled=True)
    outs = call(
        functools.partial(finish_kernel, (directions, chans, owned, chans * groups)),
        [(width, owned)] * 3,
        [SMEM, SMEM, VMEM, VMEM],
        scratch_shapes=[pltpu.VMEM((width, LANE), jnp.float32)],
    )(penalty, basis, held, own[2])

    def back(array):
        return jnp.transpose(array.reshape(2, directions, chans, owned), (3, 0, 1, 2))

    return tuple(back(array) for array in outs)


def solution(mesh):
    placed = (
        P(None, "chan", "bl"),
        P(None, None, "chan", "bl"),
        P(None, "bl"),
        P("bl", None, None, "chan"),
        P("bl", None, None, "chan"),
        P("bl", None, None, "chan"),
        P(),
    )
    return jax.shard_map(
        local,
        mesh=mesh,
        in_specs=placed,
        out_specs=(
            P("bl", None, None, "chan"),
            P("bl", None, None, "chan"),
            P("bl", None, None, "chan"),
        ),
        check_vma=False,
    )
```
